32 devices in a mesh: groups: 2 (over x), cells: 16 (over z, y, core).
Axes of the slice: x: 2, y: 2, z: 4, core: 2. Of those that a mesh axis runs over, the one named last changes fastest.
Arguments:
- features: float32 [64, 131072], P(None, ('groups', 'cells')), parts along dimension 1, may hold values from -6 to 6
- weights: float32 [131072], P(('groups', 'cells')), parts along dimension 0, may hold values from 0.5 to 2
- scales: float32 [131072], P(('groups', 'cells')), parts along dimension 0, may hold values from 0.5 to 2
- neighbors: int32 [8, 512], P(None, 'cells'), may hold values from -1 to 511, as said below
Outputs:
- log_scales: float32 [131072], P(('groups', 'cells')), parts along dimension 0
The draws below stay inside these ranges and needn't reach their ends.
There are 2 independent parts, one for each index of `groups`. The reference program is written for one: setup_inputs(seed, part) draws one part's arguments, and reference() takes and returns one part's arrays. A program takes and returns all parts, laid end to end along the dimension named above; an argument that names none is the same for every part. Nothing has to cross between parts.
Inputs may be any that keep to these rules, and one draw needn't show every extreme that they name: `neighbors`: for a block of snapshot s < 3 held by position q of its slab of 4 devices, live entries name blocks of snapshot s + 1 held by positions q - 1, q or q + 1 of the next slab; a block named at position q - 1 is among the last (33) // 2 blocks of that device, one named at position q + 1 among its first (33) // 2; slot 0 names the block at the same place in the next snapshot (index + 128); live slots come first, every such block has at least one, the first block of every device has all 8; blocks of snapshot 4 - 1 have none; entries may repeat.
All inputs are finite; a program needn't handle non-finite values.
Results may differ from the reference program's by a relative error of at most 0.0001.
Values sent between devices are 32-bit elements; how exact they have to be, the bound alone decides.
A program may use at most 64 MiB of HBM per device.

```python
import math
import jax
import jax.numpy as jnp
from jax import lax

FEATURE_DIMS = 64
BLK = 128
NBR = 8
S = 4
BPD = 32
SLAB = 4
BLOCKS_ALL = 512
CELLS_ALL = 65536


def draw_neighbors(key, part):
    key = jax.random.fold_in(key, 7)
    key_step, key_local, key_count = jax.random.split(key, 3)
    block_ids = jnp.arange(BLOCKS_ALL, dtype=jnp.int32)
    device_ids = block_ids // BPD
    snapshot = device_ids // SLAB
    position = device_ids % SLAB
    reach_blocks = (BPD + 1) // 2
    step_off = jax.random.randint(key_step, (NBR, BLOCKS_ALL), -1, 2, dtype=jnp.int32)
    new_pos = jnp.clip(position[None, :] + step_off, 0, SLAB - 1)
    actual_off = new_pos - position[None, :]
    local_ids = jax.random.randint(key_local, (NBR, BLOCKS_ALL), 0, BPD, dtype=jnp.int32)
    local_ids = jnp.where(actual_off < 0, BPD - reach_blocks + local_ids % reach_blocks, local_ids)
    local_ids = jnp.where(actual_off > 0, local_ids % reach_blocks, local_ids)
    target = ((snapshot[None, :] + 1) * SLAB + new_pos) * BPD + local_ids
    target = target.at[0].set(block_ids + SLAB * BPD)
    counts = jax.random.randint(key_count, (BLOCKS_ALL,), 1, NBR + 1, dtype=jnp.int32)
    counts = jnp.where(block_ids % BPD == 0, NBR, counts)
    slot_ids = jnp.arange(NBR, dtype=jnp.int32)[:, None]
    usable = (slot_ids < counts[None, :]) & (snapshot < S - 1)[None, :]
    return jnp.where(usable, target, -1).astype(jnp.int32)


def block_levels(own_key, dims, pieces, smallest, top_value):
    def one(axis_at, parts):
        heights = jax.random.uniform(jax.random.fold_in(jax.random.fold_in(own_key, 6), axis_at), (parts,), jnp.float32, smallest / len(pieces), top_value / len(pieces))
        return jnp.repeat(jnp.exp(heights), dims[axis_at] // parts).reshape((-1,) + (1,) * (len(dims) - axis_at - 1))

    level = one(*pieces[0])
    for cut in pieces[1:]:
        level = level * one(*cut)
    return level


def normal_values(own_key, shape, spread, most, cuts=(), held_as=jnp.bfloat16):
    level = block_levels(own_key, shape, cuts, -0.22, 0.18) if cuts else 1.0
    entries = jax.random.normal(own_key, shape, jnp.float32) * spread * level
    return jnp.minimum(jnp.maximum(entries, -most), most).astype(held_as)


def setup_inputs(seed: int = 0, part: int = 0) -> dict:
    key_list = jax.random.split(jax.random.key(seed), 5)
    own_keys = jax.random.split(jax.random.fold_in(key_list[4], part), 5)
    features = normal_values(own_keys[0], (FEATURE_DIMS, CELLS_ALL), 1.0, 6.0, ((1, 16),), jnp.float32)
    weights = jnp.clip(jnp.exp(math.log(2.0) - 1.3862944 * jax.random.uniform(own_keys[1], (CELLS_ALL,), jnp.float32) ** block_levels(own_keys[1], (CELLS_ALL,), ((0, 16),), -0.2, 0.2)), 0.5, 2.0)
    scales = jnp.clip(jnp.exp(math.log(2.0) - 1.3862944 * jax.random.uniform(own_keys[2], (CELLS_ALL,), jnp.float32) ** block_levels(own_keys[2], (CELLS_ALL,), ((0, 16),), -0.2, 0.2)), 0.5, 2.0)
    neighbors = draw_neighbors(jax.random.fold_in(key_list[4], 71), part)
    return dict(features=features, weights=weights, scales=scales, neighbors=neighbors)


def reference(features, weights, scales, neighbors):
    entropy_epsilon = FEATURE_DIMS * 0.25
    per_snap = SLAB * BPD
    blocks = features.reshape(FEATURE_DIMS, BLOCKS_ALL, BLK)
    norms = jnp.sum(blocks * blocks, axis=0)
    live_mask = neighbors >= 0
    safe_ids = jnp.where(live_mask, neighbors, 0).astype(jnp.int32)
    active_weight = live_mask.astype(jnp.float32)

    def tiles_of(block_id):
        own_feats = lax.dynamic_index_in_dim(blocks, block_id, 1, keepdims=False)
        own_norms = lax.dynamic_index_in_dim(norms, block_id, 0, keepdims=False)
        destination_index = lax.dynamic_index_in_dim(safe_ids, block_id, 1, keepdims=False)
        active_flags = lax.dynamic_index_in_dim(active_weight, block_id, 1, keepdims=False)
        other_feats = blocks[:, destination_index, :]
        other_norms = norms[destination_index]
        cross = jnp.einsum("fi,fkj->kij", own_feats, other_feats, precision=lax.Precision.HIGHEST)
        squared_distance = own_norms[None, :, None] + other_norms[:, None, :] - 2.0 * cross
        return jnp.exp(-squared_distance / entropy_epsilon) * active_flags[:, None, None], destination_index

    scale_blocks = scales.reshape(BLOCKS_ALL, BLK)
    beta = jnp.ones((BLOCKS_ALL, BLK), jnp.float32)
    for snap in range(S - 2, -1, -1):
        values = scale_blocks * beta

        def back_one(block_id):
            tiles, destination_index = tiles_of(block_id)
            return jnp.einsum("kij,kj->i", tiles, values[destination_index], precision=lax.Precision.HIGHEST)

        ids_here = jnp.arange(snap * per_snap, (snap + 1) * per_snap, dtype=jnp.int32)
        beta = beta.at[snap * per_snap:(snap + 1) * per_snap].set(lax.map(back_one, ids_here))

    phi = jnp.ones((BLOCKS_ALL, BLK), jnp.float32)
    for snap in range(S - 1):
        values = scale_blocks * phi

        def fore_one(block_id):
            tiles, destination_index = tiles_of(block_id)
            own_vals = lax.dynamic_index_in_dim(values, block_id, 0, keepdims=False)
            return jnp.einsum("kij,i->kj", tiles, own_vals, precision=lax.Precision.HIGHEST)

        ids_here = jnp.arange(snap * per_snap, (snap + 1) * per_snap, dtype=jnp.int32)
        contrib = lax.map(fore_one, ids_here)
        targets = safe_ids[:, snap * per_snap:(snap + 1) * per_snap].T
        summed = jax.ops.segment_sum(contrib.reshape(-1, BLK), targets.reshape(-1), num_segments=BLOCKS_ALL)
        phi = phi.at[(snap + 1) * per_snap:(snap + 2) * per_snap].set(summed[(snap + 1) * per_snap:(snap + 2) * per_snap])

    return jnp.log(weights) - jnp.log(phi.reshape(-1)) - jnp.log(beta.reshape(-1))
```

```python
import functools
import jax
import jax.numpy as jnp
from jax import lax
from jax.experimental import pallas as pl
from jax.experimental.pallas import tpu as pltpu
from jax.sharding import PartitionSpec as P

S = 4
LOG2E = 1.4426950408889634


def from_next(block, slab, offset):
    n = lax.axis_size("cells")
    route = [
        (i + slab + offset, i)
        for i in range(n - slab)
        if 0 <= i % slab + offset < slab
    ]
    return lax.ppermute(block, "cells", route)


def to_next(block, slab, offset):
    n = lax.axis_size("cells")
    route = [
        (i, i + slab + offset)
        for i in range(n - slab)
        if 0 <= i % slab + offset < slab
    ]
    return lax.ppermute(block, "cells", route)


def split(x):
    hi = x.astype(jnp.bfloat16)
    lo = (x - hi.astype(jnp.float32)).astype(jnp.bfloat16)
    return hi, lo


def stacked(x, eps, own):
    norm = jnp.sum(x * x, axis=0, keepdims=True) * (-LOG2E / eps)
    a = norm.astype(jnp.bfloat16).astype(jnp.float32)
    b = (norm - a).astype(jnp.bfloat16).astype(jnp.float32)
    c = norm - a - b
    row = lax.broadcasted_iota(jnp.int32, (16, x.shape[1]), 0)
    if not own:
        row = row - 3
    tail = jnp.where(row == 0, a, jnp.where(row == 1, b, jnp.where(row == 2, c, 0.0)))
    ones = (row >= 3) & (row < 6) if own else (row < 0)
    tail = jnp.where(ones, 1.0, tail).astype(jnp.bfloat16)
    hi, lo = split(x * (2.0 * LOG2E / eps) if own else x)
    parts = [hi, lo, hi, tail] if own else [hi, hi, lo, tail]
    return jnp.concatenate(parts, axis=0)


def sweep_block(b, slots, ids, live, tile, values, weighted, message, partial):
    blk = message.shape[1]
    column = jnp.broadcast_to(weighted[pl.ds(b, 1), :], (blk, blk)).T
    acc = jnp.zeros((blk, blk), jnp.float32)
    for k in range(slots):
        at = ids[k, b]
        k_tile = tile(k)
        acc = acc + k_tile * values[pl.ds(at, 1), :]
        out = jnp.sum(k_tile * column, axis=0, keepdims=True)
        partial[pl.ds(at, 1), :] += out
    ones = jnp.ones((8, blk), jnp.float32)
    rows = lax.dot_general(
        ones, acc, (((1,), (1,)), ((), ())),
        precision=lax.Precision.HIGHEST, preferred_element_type=jnp.float32,
    )
    message[pl.ds(b, 1), :] = rows[0:1]


def first_kernel(eps, ids, live, below, same, above, feats, values, weighted,
                 tiles, message, partial, stack):
    b = pl.program_id(0)
    slots = ids.shape[0]
    blk = message.shape[1]

    @pl.when(b == 0)
    def _():
        partial[...] = jnp.zeros_like(partial)
        base = 0
        for piece in (below, same, above):
            count = piece.shape[1] // blk

            def prepare(w, _, piece=piece, base=base):
                x = piece[:, pl.ds(pl.multiple_of(w * blk, blk), blk)]
                stack[base + w] = stacked(x, eps, False)
                return 0

            lax.fori_loop(0, count, prepare, 0)
            base += count

    mine = stacked(feats[...], eps, True).T

    def tile(k):
        expo = lax.dot_general(
            mine, stack[ids[k, b]], (((1,), (0,)), ((), ())),
            preferred_element_type=jnp.float32,
        )
        result = jnp.exp2(expo) * live[k, b].astype(jnp.float32)
        tiles[0, :, k * blk : (k + 1) * blk] = result
        return result

    sweep_block(b, slots, ids, live, tile, values, weighted, message, partial)


def next_kernel(ids, live, tiles, values, weighted, message, partial):
    b = pl.program_id(0)
    blk = message.shape[1]

    @pl.when(b == 0)
    def _():
        partial[...] = jnp.zeros_like(partial)

    def tile(k):
        return tiles[0, :, k * blk : (k + 1) * blk]

    sweep_block(b, ids.shape[0], ids, live, tile, values, weighted, message, partial)


def local(features, weights, scales, neighbors):
    dims = features.shape[0]
    slots, own = neighbors.shape
    blk = features.shape[1] // own
    reach = (own + 1) // 2
    wide = own + 2 * reach
    slab = lax.axis_size("cells") // S
    me = lax.axis_index("cells")
    place = me // slab
    eps = dims * 0.25

    live = (neighbors >= 0).astype(jnp.int32)
    first = (me + slab) * own - reach
    ids = jnp.where(neighbors >= 0, neighbors - first, 0)
    ids = jnp.clip(ids, 0, wide - 1)

    same = from_next(features, slab, 0)
    below = from_next(features[:, (own - reach) * blk :], slab, -1)
    above = from_next(features[:, : reach * blk], slab, 1)

    scale = scales.reshape(own, blk)

    def window(values):
        return jnp.concatenate(
            [
                from_next(values[own - reach :], slab, -1),
                from_next(values, slab, 0),
                from_next(values[:reach], slab, 1),
            ],
            axis=0,
        )

    smem = pl.BlockSpec(memory_space=pltpu.SMEM)
    vmem = pl.BlockSpec(memory_space=pltpu.VMEM)
    tile_spec = pl.BlockSpec((1, blk, slots * blk), lambda b: (b, 0, 0))
    rows = jax.ShapeDtypeStruct((own, blk), jnp.float32)
    sums = jax.ShapeDtypeStruct((wide, blk), jnp.float32)
    params = pltpu.CompilerParams(vmem_limit_bytes=32 * 1024 * 1024)

    tiles, message, partial = pl.pallas_call(
        functools.partial(first_kernel, eps),
        grid=(own,),
        in_specs=[smem, smem, vmem, vmem, vmem,
                  pl.BlockSpec((dims, blk), lambda b: (0, b)), vmem, vmem],
        out_specs=[tile_spec, vmem, vmem],
        out_shape=[
            jax.ShapeDtypeStruct((own, blk, slots * blk), jnp.float32), rows, sums,
        ],
        scratch_shapes=[pltpu.VMEM((wide, 3 * dims + 16, blk), jnp.bfloat16)],
        compiler_params=params,
    )(ids, live, below, same, above, features, window(scale), scale)

    def settle(message, partial):
        beta = jnp.where(place == S - 1, 1.0, message)
        total = to_next(partial[reach : reach + own], slab, 0)
        low = to_next(partial[:reach], slab, -1)
        high = to_next(partial[reach + own :], slab, 1)
        total = total.at[own - reach :].add(low)
        total = total.at[:reach].add(high)
        phi = jnp.where(place == 0, 1.0, total)
        return beta, phi

    beta, phi = settle(message, partial)
    for _ in range(S - 2):
        message, partial = pl.pallas_call(
            next_kernel,
            grid=(own,),
            in_specs=[smem, smem, tile_spec, vmem, vmem],
            out_specs=[vmem, vmem],
            out_shape=[rows, sums],
            compiler_params=params,
        )(ids, live, tiles, window(scale * beta), scale * phi)
        beta, phi = settle(message, partial)
    return jnp.log(weights) - jnp.log(phi.reshape(-1)) - jnp.log(beta.reshape(-1))


def solution(mesh):
    placed = (
        P(None, ("groups", "cells")),
        P(("groups", "cells")),
        P(("groups", "cells")),
        P(None, "cells"),
    )
    return jax.shard_map(
        local, mesh=mesh, in_specs=placed, out_specs=P(("groups", "cells")), check_vma=False
    )
```

```python
import functools
import jax
import jax.numpy as jnp
from jax import lax
from jax.experimental import pallas as pl
from jax.experimental.pallas import tpu as pltpu
from jax.sharding import PartitionSpec as P

S = 4
LOG2E = 1.4426950408889634


def from_next(block, slab, offset):
    n = lax.axis_size("cells")
    route = [
        (i + slab + offset, i)
        for i in range(n - slab)
        if 0 <= i % slab + offset < slab
    ]
    return lax.ppermute(block, "cells", route)


def split(x):
    hi = x.astype(jnp.bfloat16)
    lo = (x - hi.astype(jnp.float32)).astype(jnp.bfloat16)
    return hi, lo


def stacked(x, eps, own):
    norm = jnp.sum(x * x, axis=0, keepdims=True) * (-LOG2E / eps)
    a = norm.astype(jnp.bfloat16).astype(jnp.float32)
    b = (norm - a).astype(jnp.bfloat16).astype(jnp.float32)
    c = norm - a - b
    row = lax.broadcasted_iota(jnp.int32, (16, x.shape[1]), 0)
    if not own:
        row = row - 3
    tail = jnp.where(row == 0, a, jnp.where(row == 1, b, jnp.where(row == 2, c, 0.0)))
    ones = (row >= 3) & (row < 6) if own else (row < 0)
    tail = jnp.where(ones, 1.0, tail).astype(jnp.bfloat16)
    hi, lo = split(x * (2.0 * LOG2E / eps) if own else x)
    parts = [hi, lo, hi, tail] if own else [hi, hi, lo, tail]
    return jnp.concatenate(parts, axis=0)


def sweep_block(b, slots, ids, live, tile, values, weighted, message, partial):
    blk = message.shape[1]
    column = jnp.broadcast_to(weighted[pl.ds(b, 1), :], (blk, blk)).T
    acc = jnp.zeros((blk, blk), jnp.float32)
    for k in range(slots):
        at = ids[k, b]
        k_tile = tile(k)
        acc = acc + k_tile * values[pl.ds(at, 1), :]
        out = jnp.sum(k_tile * column, axis=0, keepdims=True)
        partial[pl.ds(at, 1), :] += out
    ones = jnp.ones((8, blk), jnp.float32)
    rows = lax.dot_general(
        ones, acc, (((1,), (1,)), ((), ())),
        precision=lax.Precision.HIGHEST, preferred_element_type=jnp.float32,
    )
    message[pl.ds(b, 1), :] = rows[0:1]


def first_kernel(eps, ids, live, below, same, above, feats, values, weighted,
                 tiles, message, partial, stack):
    b = pl.program_id(0)
    slots = ids.shape[0]
    blk = message.shape[1]

    @pl.when(b == 0)
    def _():
        partial[...] = jnp.zeros_like(partial)
        base = 0
        for piece in (below, same, above):
            count = piece.shape[1] // blk

            def prepare(w, _, piece=piece, base=base):
                x = piece[:, pl.ds(pl.multiple_of(w * blk, blk), blk)]
                stack[base + w] = stacked(x, eps, False)
                return 0

            lax.fori_loop(0, count, prepare, 0)
            base += count

    mine = stacked(feats[...], eps, True).T

    def tile(k):
        expo = lax.dot_general(
            mine, stack[ids[k, b]], (((1,), (0,)), ((), ())),
            preferred_element_type=jnp.float32,
        )
        result = jnp.exp2(expo) * live[k, b].astype(jnp.float32)
        tiles[0, :, k * blk : (k + 1) * blk] = result
        return result

    sweep_block(b, slots, ids, live, tile, values, weighted, message, partial)


def chain_kernel(slab, ids, hot, tiles, scale, message0, partial0, beta, phi,
                 window, vals, part, same_in, low_in, high_in, contrib,
                 vsend, vrecv, psend, precv):
    me = lax.axis_index("cells")
    place, spot = me // slab, me % slab
    slots = ids.shape[0]
    own, blk = scale.shape
    wide = window.shape[0]
    reach = (wide - own) // 2
    inside = (spot > 0, spot >= 0, spot < slab - 1)

    window[...] = jnp.zeros_like(window)
    low_in[...] = jnp.zeros_like(low_in)
    high_in[...] = jnp.zeros_like(high_in)
    vals[...] = scale[...] * message0[...]
    part[...] = partial0[...]

    barrier = pltpu.get_barrier_semaphore()
    for near, step in ((place > 0, -slab), (place < S - 1, slab)):
        for o in (-1, 0, 1):
            @pl.when(near & inside[o + 1])
            def _(step=step, o=o):
                pl.semaphore_signal(
                    barrier, inc=1, device_id={"cells": me + step + o},
                    device_id_type=pl.DeviceIdType.MESH,
                )
    sides = jnp.where(place > 0, 1, 0) + jnp.where(place < S - 1, 1, 0)
    near = 1 + jnp.where(inside[0], 1, 0) + jnp.where(inside[2], 1, 0)
    pl.semaphore_wait(barrier, sides * near)

    def copy(src, dst, send, recv, target):
        return pltpu.make_async_remote_copy(
            src_ref=src, dst_ref=dst, send_sem=send, recv_sem=recv,
            device_id={"cells": target}, device_id_type=pl.DeviceIdType.MESH,
        )

    value_parts = {
        -1: (vals.at[pl.ds(0, reach)], window.at[pl.ds(reach + own, reach)]),
        0: (vals, window.at[pl.ds(reach, own)]),
        1: (vals.at[pl.ds(own - reach, reach)], window.at[pl.ds(0, reach)]),
    }
    sum_parts = {
        -1: (part.at[pl.ds(0, reach)], low_in),
        0: (part.at[pl.ds(reach, own)], same_in),
        1: (part.at[pl.ds(reach + own, reach)], high_in),
    }

    def value_copy(o):
        src, dst = value_parts[o]
        return copy(src, dst, vsend.at[o + 1], vrecv.at[o + 1], me - slab + o)

    def sum_copy(o):
        src, dst = sum_parts[o]
        return copy(src, dst, psend.at[o + 1], precv.at[o + 1], me + slab + o)

    def each(cond, make, act, flip=False):
        for o in (-1, 0, 1):
            @pl.when(cond & inside[(-o if flip else o) + 1])
            def _(o=o):
                getattr(make(o), act)()

    each(place == 2, value_copy, "start")
    each(place == 0, sum_copy, "start")
    each(place <= 1, value_copy, "wait_recv", True)
    each(place >= 1, sum_copy, "wait_recv", True)

    @pl.when(place >= 1)
    def _():
        phi[...] = same_in[...]
        phi[pl.ds(own - reach, reach), :] += low_in[...]
        phi[pl.ds(0, reach), :] += high_in[...]

    @pl.when(place == 0)
    def _():
        phi[...] = jnp.ones_like(phi)

    @pl.when(place == S - 1)
    def _():
        beta[...] = jnp.ones_like(beta)

    @pl.when(place == S - 2)
    def _():
        beta[...] = message0[...]

    @pl.when(place <= 1)
    def _():
        def back(b, _):
            acc = jnp.zeros((blk, blk), jnp.float32)
            for k in range(slots):
                row = window[pl.ds(ids[k, b], 1), :]
                acc = acc + tiles[b, :, k * blk : (k + 1) * blk] * row
            rows = lax.dot_general(
                jnp.ones((8, blk), jnp.float32), acc, (((1,), (1,)), ((), ())),
                precision=lax.Precision.HIGHEST, preferred_element_type=jnp.float32,
            )
            beta[pl.ds(b, 1), :] = rows[0:1]
            return 0

        lax.fori_loop(0, own, back, 0)

    @pl.when(place == 1)
    def _():
        vals[...] = scale[...] * beta[...]

    each(place == 1, value_copy, "start")

    @pl.when((place >= 1) & (place < S - 1))
    def _():
        def fore(b, _):
            weighted = scale[pl.ds(b, 1), :] * phi[pl.ds(b, 1), :]
            column = jnp.broadcast_to(weighted, (blk, blk)).T
            for k in range(slots):
                out = tiles[b, :, k * blk : (k + 1) * blk] * column
                contrib[b, k : k + 1, :] = jnp.sum(out, axis=0, keepdims=True)
            return 0

        lax.fori_loop(0, own, fore, 0)
        part[...] = lax.dot_general(
            hot[...], contrib[...].reshape(own * slots, blk), (((1,), (0,)), ((), ())),
            precision=lax.Precision.HIGHEST, preferred_element_type=jnp.float32,
        )

    late = (place >= 1) & (place < S - 1)
    each(late, sum_copy, "start")
    each(late, value_copy, "wait_send")
    each(place < S - 1, sum_copy, "wait_send")


def local(features, weights, scales, neighbors):
    dims = features.shape[0]
    slots, own = neighbors.shape
    blk = features.shape[1] // own
    reach = (own + 1) // 2
    wide = own + 2 * reach
    slab = lax.axis_size("cells") // S
    me = lax.axis_index("cells")
    place = me // slab
    eps = dims * 0.25

    live = (neighbors >= 0).astype(jnp.int32)
    first = (me + slab) * own - reach
    ids = jnp.where(neighbors >= 0, neighbors - first, 0)
    ids = jnp.clip(ids, 0, wide - 1)

    same = from_next(features, slab, 0)
    below = from_next(features[:, (own - reach) * blk :], slab, -1)
    above = from_next(features[:, : reach * blk], slab, 1)

    scale = scales.reshape(own, blk)

    def window(values):
        return jnp.concatenate(
            [
                from_next(values[own - reach :], slab, -1),
                from_next(values, slab, 0),
                from_next(values[:reach], slab, 1),
            ],
            axis=0,
        )

    smem = pl.BlockSpec(memory_space=pltpu.SMEM)
    vmem = pl.BlockSpec(memory_space=pltpu.VMEM)
    tile_spec = pl.BlockSpec((1, blk, slots * blk), lambda b: (b, 0, 0))
    rows = jax.ShapeDtypeStruct((own, blk), jnp.float32)
    sums = jax.ShapeDtypeStruct((wide, blk), jnp.float32)
    params = pltpu.CompilerParams(vmem_limit_bytes=32 * 1024 * 1024)

    tiles, message, partial = pl.pallas_call(
        functools.partial(first_kernel, eps),
        grid=(own,),
        in_specs=[smem, smem, vmem, vmem, vmem,
                  pl.BlockSpec((dims, blk), lambda b: (0, b)), vmem, vmem],
        out_specs=[tile_spec, vmem, vmem],
        out_shape=[
            jax.ShapeDtypeStruct((own, blk, slots * blk), jnp.float32), rows, sums,
        ],
        scratch_shapes=[pltpu.VMEM((wide, 3 * dims + 16, blk), jnp.bfloat16)],
        compiler_params=params,
    )(ids, live, below, same, above, features, window(scale), scale)

    at = ids.T.reshape(1, own * slots)
    hot = (at == jnp.arange(wide, dtype=jnp.int32)[:, None]) & (
        live.T.reshape(1, own * slots) > 0
    )
    sem = pltpu.SemaphoreType.DMA((3,))
    beta, phi = pl.pallas_call(
        functools.partial(chain_kernel, slab),
        in_specs=[smem] + [vmem] * 5,
        out_specs=[vmem, vmem],
        out_shape=[rows, rows],
        scratch_shapes=[
            pltpu.VMEM((wide, blk), jnp.float32),
            pltpu.VMEM((own, blk), jnp.float32),
            pltpu.VMEM((wide, blk), jnp.float32),
            pltpu.VMEM((own, blk), jnp.float32),
            pltpu.VMEM((reach, blk), jnp.float32),
            pltpu.VMEM((reach, blk), jnp.float32),
            pltpu.VMEM((own, slots, blk), jnp.float32),
            sem, sem, sem, sem,
        ],
        compiler_params=pltpu.CompilerParams(
            collective_id=0, has_side_effects=True, vmem_limit_bytes=40 * 1024 * 1024
        ),
    )(ids, hot.astype(jnp.float32), tiles, scale, message, partial)
    return jnp.log(weights) - jnp.log(phi.reshape(-1)) - jnp.log(beta.reshape(-1))


def solution(mesh):
    placed = (
        P(None, ("groups", "cells")),
        P(("groups", "cells")),
        P(("groups", "cells")),
        P(None, "cells"),
    )
    return jax.shard_map(
        local, mesh=mesh, in_specs=placed, out_specs=P(("groups", "cells")), check_vma=False
    )
```

```python
import functools
import jax
import jax.numpy as jnp
from jax import lax
from jax.experimental import pallas as pl
from jax.experimental.pallas import tpu as pltpu
from jax.sharding import PartitionSpec as P

S = 4
LOG2E = 1.4426950408889634


def split(x):
    hi = x.astype(jnp.bfloat16)
    lo = (x - hi.astype(jnp.float32)).astype(jnp.bfloat16)
    return hi, lo


def stacked(x, eps, own):
    norm = jnp.sum(x * x, axis=0, keepdims=True) * (-LOG2E / eps)
    a = norm.astype(jnp.bfloat16).astype(jnp.float32)
    b = (norm - a).astype(jnp.bfloat16).astype(jnp.float32)
    c = norm - a - b
    row = lax.broadcasted_iota(jnp.int32, (16, x.shape[1]), 0)
    if not own:
        row = row - 3
    tail = jnp.where(row == 0, a, jnp.where(row == 1, b, jnp.where(row == 2, c, 0.0)))
    ones = (row >= 3) & (row < 6) if own else (row < 0)
    tail = jnp.where(ones, 1.0, tail).astype(jnp.bfloat16)
    hi, lo = split(x * (2.0 * LOG2E / eps) if own else x)
    parts = [hi, lo, hi, tail] if own else [hi, hi, lo, tail]
    return jnp.concatenate(parts, axis=0)


def chain_kernel(slab, eps, ids, live, feats, hot, scale, beta, phi,
                 tiles, fwin, stack,
                 window, vals, part, same_in, low_in, high_in, contrib,
                 fsend, frecv, vsend, vrecv, psend, precv):
    me = lax.axis_index("cells")
    place, spot = me // slab, me % slab
    slots = ids.shape[0]
    own, blk = scale.shape
    wide = window.shape[0]
    reach = (wide - own) // 2
    inside = (spot > 0, spot >= 0, spot < slab - 1)

    window[...] = jnp.zeros_like(window)
    low_in[...] = jnp.zeros_like(low_in)
    high_in[...] = jnp.zeros_like(high_in)
    vals[...] = scale[...]
    edge, middle = reach * blk, own * blk
    fwin[:, :edge] = jnp.zeros((fwin.shape[0], edge), jnp.float32)
    fwin[:, edge + middle :] = jnp.zeros((fwin.shape[0], edge), jnp.float32)

    barrier = pltpu.get_barrier_semaphore()
    for near, step in ((place > 0, -slab), (place < S - 1, slab)):
        for o in (-1, 0, 1):
            @pl.when(near & inside[o + 1])
            def _(step=step, o=o):
                pl.semaphore_signal(
                    barrier, inc=1, device_id={"cells": me + step + o},
                    device_id_type=pl.DeviceIdType.MESH,
                )
    sides = jnp.where(place > 0, 1, 0) + jnp.where(place < S - 1, 1, 0)
    near = 1 + jnp.where(inside[0], 1, 0) + jnp.where(inside[2], 1, 0)
    pl.semaphore_wait(barrier, sides * near)

    def copy(src, dst, send, recv, target):
        return pltpu.make_async_remote_copy(
            src_ref=src, dst_ref=dst, send_sem=send, recv_sem=recv,
            device_id={"cells": target}, device_id_type=pl.DeviceIdType.MESH,
        )

    value_parts = {
        -1: (vals.at[pl.ds(0, reach)], window.at[pl.ds(reach + own, reach)]),
        0: (vals, window.at[pl.ds(reach, own)]),
        1: (vals.at[pl.ds(own - reach, reach)], window.at[pl.ds(0, reach)]),
    }
    sum_parts = {
        -1: (part.at[pl.ds(0, reach)], low_in),
        0: (part.at[pl.ds(reach, own)], same_in),
        1: (part.at[pl.ds(reach + own, reach)], high_in),
    }

    feature_parts = {
        -1: (feats.at[:, pl.ds(0, edge)], fwin.at[:, pl.ds(edge + middle, edge)]),
        0: (feats, fwin.at[:, pl.ds(edge, middle)]),
        1: (feats.at[:, pl.ds(middle - edge, edge)], fwin.at[:, pl.ds(0, edge)]),
    }

    def feature_copy(o):
        src, dst = feature_parts[o]
        return copy(src, dst, fsend.at[o + 1], frecv.at[o + 1], me - slab + o)

    def value_copy(o):
        src, dst = value_parts[o]
        return copy(src, dst, vsend.at[o + 1], vrecv.at[o + 1], me - slab + o)

    def sum_copy(o):
        src, dst = sum_parts[o]
        return copy(src, dst, psend.at[o + 1], precv.at[o + 1], me + slab + o)

    def each(cond, make, act, flip=False):
        for o in (-1, 0, 1):
            @pl.when(cond & inside[(-o if flip else o) + 1])
            def _(o=o):
                getattr(make(o), act)()

    each(place >= 1, feature_copy, "start")
    each(place == S - 1, value_copy, "start")
    has_next = place < S - 1
    each(has_next, feature_copy, "wait_recv", True)

    def lanes(b):
        return pl.ds(pl.multiple_of(b * blk, blk), blk)

    @pl.when(has_next)
    def _():
        def prepare(w, _):
            stack[w] = stacked(fwin[:, lanes(w)], eps, False)
            return 0

        lax.fori_loop(0, wide, prepare, 0)

        def build(b, _):
            mine = stacked(feats[:, lanes(b)], eps, True).T
            for k in range(0, slots, 2):
                theirs = jnp.concatenate(
                    [stack[ids[k, b]], stack[ids[k + 1, b]]], axis=1
                )
                expo = lax.dot_general(
                    mine, theirs, (((1,), (0,)), ((), ())),
                    preferred_element_type=jnp.float32,
                )
                tile = jnp.exp2(expo)
                for i in (0, 1):
                    tiles[b, :, (k + i) * blk : (k + i + 1) * blk] = (
                        tile[:, i * blk : (i + 1) * blk] * live[k + i, b]
                    )
            return 0

        lax.fori_loop(0, own, build, 0)

    def forward(cond):
        @pl.when(cond)
        def _():
            def fore(b, _):
                weighted = scale[pl.ds(b, 1), :] * phi[pl.ds(b, 1), :]
                column = jnp.broadcast_to(weighted, (blk, blk)).T
                for k in range(slots):
                    out = tiles[b, :, k * blk : (k + 1) * blk] * column
                    contrib[b, k : k + 1, :] = jnp.sum(out, axis=0, keepdims=True)
                return 0

            lax.fori_loop(0, own, fore, 0)
            part[...] = lax.dot_general(
                hot[...], contrib[...].reshape(own * slots, blk),
                (((1,), (0,)), ((), ())),
                precision=lax.Precision.HIGHEST, preferred_element_type=jnp.float32,
            )

        each(cond, sum_copy, "start")

    @pl.when(place == 0)
    def _():
        phi[...] = jnp.ones_like(phi)

    @pl.when(place == S - 1)
    def _():
        beta[...] = jnp.ones_like(beta)

    forward(place == 0)
    each(has_next, value_copy, "wait_recv", True)

    @pl.when(has_next)
    def _():
        def back(b, _):
            acc = jnp.zeros((blk, blk), jnp.float32)
            for k in range(slots):
                row = window[pl.ds(ids[k, b], 1), :]
                acc = acc + tiles[b, :, k * blk : (k + 1) * blk] * row
            rows = lax.dot_general(
                jnp.ones((8, blk), jnp.float32), acc, (((1,), (1,)), ((), ())),
                precision=lax.Precision.HIGHEST, preferred_element_type=jnp.float32,
            )
            beta[pl.ds(b, 1), :] = rows[0:1]
            return 0

        lax.fori_loop(0, own, back, 0)
        vals[...] = scale[...] * beta[...]

    each((place >= 1) & has_next, value_copy, "start")
    each(place >= 1, sum_copy, "wait_recv", True)

    @pl.when(place >= 1)
    def _():
        phi[...] = same_in[...]
        phi[pl.ds(own - reach, reach), :] += low_in[...]
        phi[pl.ds(0, reach), :] += high_in[...]

    forward((place >= 1) & has_next)
    each(place >= 1, feature_copy, "wait_send")
    each(place >= 1, value_copy, "wait_send")
    each(has_next, sum_copy, "wait_send")


def local(features, weights, scales, neighbors):
    dims = features.shape[0]
    slots, own = neighbors.shape
    blk = features.shape[1] // own
    reach = (own + 1) // 2
    wide = own + 2 * reach
    slab = lax.axis_size("cells") // S
    me = lax.axis_index("cells")
    eps = dims * 0.25

    live = (neighbors >= 0).astype(jnp.float32)
    first = (me + slab) * own - reach
    ids = jnp.where(neighbors >= 0, neighbors - first, reach)
    ids = jnp.clip(ids, 0, wide - 1)

    scale = scales.reshape(own, blk)
    smem = pl.BlockSpec(memory_space=pltpu.SMEM)
    vmem = pl.BlockSpec(memory_space=pltpu.VMEM)
    rows = jax.ShapeDtypeStruct((own, blk), jnp.float32)
    at = ids.T.reshape(1, own * slots)
    hot = (at == jnp.arange(wide, dtype=jnp.int32)[:, None]) & (
        live.T.reshape(1, own * slots) > 0
    )
    sem = pltpu.SemaphoreType.DMA((3,))
    beta, phi = pl.pallas_call(
        functools.partial(chain_kernel, slab, eps),
        in_specs=[smem] * 2 + [vmem] * 3,
        out_specs=[vmem, vmem],
        out_shape=[rows, rows],
        scratch_shapes=[
            pltpu.VMEM((own, blk, slots * blk), jnp.float32),
            pltpu.VMEM((dims, wide * blk), jnp.float32),
            pltpu.VMEM((wide, 3 * dims + 16, blk), jnp.bfloat16),
            pltpu.VMEM((wide, blk), jnp.float32),
            pltpu.VMEM((own, blk), jnp.float32),
            pltpu.VMEM((wide, blk), jnp.float32),
            pltpu.VMEM((own, blk), jnp.float32),
            pltpu.VMEM((reach, blk), jnp.float32),
            pltpu.VMEM((reach, blk), jnp.float32),
            pltpu.VMEM((own, slots, blk), jnp.float32),
            sem, sem, sem, sem, sem, sem,
        ],
        compiler_params=pltpu.CompilerParams(
            collective_id=0, has_side_effects=True, vmem_limit_bytes=40 * 1024 * 1024
        ),
    )(ids, live, features, hot.astype(jnp.float32), scale)
    return jnp.log(weights) - jnp.log(phi.reshape(-1)) - jnp.log(beta.reshape(-1))


def solution(mesh):
    placed = (
        P(None, ("groups", "cells")),
        P(("groups", "cells")),
        P(("groups", "cells")),
        P(None, "cells"),
    )
    return jax.shard_map(
        local, mesh=mesh, in_specs=placed, out_specs=P(("groups", "cells")), check_vma=False
    )
```

```python
import functools
import jax
import jax.numpy as jnp
from jax import lax
from jax.experimental import pallas as pl
from jax.experimental.pallas import tpu as pltpu
from jax.sharding import PartitionSpec as P

S = 4
LOG2E = 1.4426950408889634


def split(x):
    hi = x.astype(jnp.bfloat16)
    lo = (x - hi.astype(jnp.float32)).astype(jnp.bfloat16)
    return hi, lo


def stacked(x, eps, own):
    norm = jnp.sum(x * x, axis=0, keepdims=True) * (-LOG2E / eps)
    a = norm.astype(jnp.bfloat16).astype(jnp.float32)
    b = (norm - a).astype(jnp.bfloat16).astype(jnp.float32)
    c = norm - a - b
    row = lax.broadcasted_iota(jnp.int32, (16, x.shape[1]), 0)
    if not own:
        row = row - 3
    tail = jnp.where(row == 0, a, jnp.where(row == 1, b, jnp.where(row == 2, c, 0.0)))
    ones = (row >= 3) & (row < 6) if own else (row < 0)
    tail = jnp.where(ones, 1.0, tail).astype(jnp.bfloat16)
    hi, lo = split(x * (2.0 * LOG2E / eps) if own else x)
    parts = [hi, lo, hi, tail] if own else [hi, hi, lo, tail]
    return jnp.concatenate(parts, axis=0)


def chain_kernel(slab, eps, ids, live, feats, hot, scale, beta, phi,
                 tiles, fwin, stack,
                 window, vals, part, same_in, low_in, high_in, contrib,
                 fsend, frecv, rsend, rrecv, vsend, vrecv, psend, precv):
    me = lax.axis_index("cells")
    place, spot = me // slab, me % slab
    slots = ids.shape[0]
    own, blk = scale.shape
    wide = window.shape[0]
    reach = (wide - own) // 2
    inside = (spot > 0, spot >= 0, spot < slab - 1)

    window[...] = jnp.zeros_like(window)
    low_in[...] = jnp.zeros_like(low_in)
    high_in[...] = jnp.zeros_like(high_in)
    vals[...] = scale[...]
    edge, middle = reach * blk, own * blk
    fwin[:, :edge] = jnp.zeros((fwin.shape[0], edge), jnp.float32)
    fwin[:, edge + middle :] = jnp.zeros((fwin.shape[0], edge), jnp.float32)

    barrier = pltpu.get_barrier_semaphore()
    for near, step in ((place > 0, -slab), (place < S - 1, slab)):
        for o in (-1, 0, 1):
            @pl.when(near & inside[o + 1])
            def _(step=step, o=o):
                pl.semaphore_signal(
                    barrier, inc=1, device_id={"cells": me + step + o},
                    device_id_type=pl.DeviceIdType.MESH,
                )
    for o in (-1, 1):
        @pl.when(inside[o + 1])
        def _(o=o):
            pl.semaphore_signal(
                barrier, inc=1, device_id={"cells": me + o},
                device_id_type=pl.DeviceIdType.MESH,
            )
    sides = jnp.where(place > 0, 1, 0) + jnp.where(place < S - 1, 1, 0)
    near = 1 + jnp.where(inside[0], 1, 0) + jnp.where(inside[2], 1, 0)
    pl.semaphore_wait(barrier, sides * near + near - 1)

    def copy(src, dst, send, recv, target):
        return pltpu.make_async_remote_copy(
            src_ref=src, dst_ref=dst, send_sem=send, recv_sem=recv,
            device_id={"cells": target}, device_id_type=pl.DeviceIdType.MESH,
        )

    value_parts = {
        -1: (vals.at[pl.ds(0, reach)], window.at[pl.ds(reach + own, reach)]),
        0: (vals, window.at[pl.ds(reach, own)]),
        1: (vals.at[pl.ds(own - reach, reach)], window.at[pl.ds(0, reach)]),
    }
    sum_parts = {
        -1: (part.at[pl.ds(0, reach)], low_in),
        0: (part.at[pl.ds(reach, own)], same_in),
        1: (part.at[pl.ds(reach + own, reach)], high_in),
    }

    def feature_copy(h):
        return copy(
            feats.at[:, pl.ds(h * edge, edge)], fwin.at[:, pl.ds((h + 1) * edge, edge)],
            fsend.at[h], frecv.at[h], me - slab,
        )

    def relay(h):
        return copy(
            fwin.at[:, pl.ds((h + 1) * edge, edge)],
            fwin.at[:, pl.ds((1 - h) * (edge + middle), edge)],
            rsend.at[h], rrecv.at[h], me + 2 * h - 1,
        )

    def value_copy(o):
        src, dst = value_parts[o]
        return copy(src, dst, vsend.at[o + 1], vrecv.at[o + 1], me - slab + o)

    def sum_copy(o):
        src, dst = sum_parts[o]
        return copy(src, dst, psend.at[o + 1], precv.at[o + 1], me + slab + o)

    def each(cond, make, act, flip=False):
        for o in (-1, 0, 1):
            @pl.when(cond & inside[(-o if flip else o) + 1])
            def _(o=o):
                getattr(make(o), act)()

    @pl.when(place >= 1)
    def _():
        feature_copy(0).start()
        feature_copy(1).start()

    each(place == S - 1, value_copy, "start")
    has_next = place < S - 1

    def lanes(b):
        return pl.ds(pl.multiple_of(b * blk, blk), blk)

    def prepare(w, _):
        stack[w] = stacked(fwin[:, lanes(w)], eps, False)
        return 0

    for h in (0, 1):
        @pl.when(has_next)
        def _(h=h):
            feature_copy(h).wait_recv()

        @pl.when(has_next & inside[2 * h])
        def _(h=h):
            relay(h).start()

        @pl.when(has_next)
        def _(h=h):
            lax.fori_loop((h + 1) * reach, (h + 2) * reach, prepare, 0)

    for h in (0, 1):
        @pl.when(has_next & inside[2 - 2 * h])
        def _(h=h):
            relay(h).wait_recv()

    @pl.when(has_next)
    def _():
        lax.fori_loop(0, reach, prepare, 0)
        lax.fori_loop(reach + own, wide, prepare, 0)

        def build(b, _):
            mine = stacked(feats[:, lanes(b)], eps, True).T
            for k in range(0, slots, 2):
                theirs = jnp.concatenate(
                    [stack[ids[k, b]], stack[ids[k + 1, b]]], axis=1
                )
                expo = lax.dot_general(
                    mine, theirs, (((1,), (0,)), ((), ())),
                    preferred_element_type=jnp.float32,
                )
                tile = jnp.exp2(expo)
                for i in (0, 1):
                    tiles[b, :, (k + i) * blk : (k + i + 1) * blk] = (
                        tile[:, i * blk : (i + 1) * blk] * live[k + i, b]
                    )
            return 0

        lax.fori_loop(0, own, build, 0)

    def forward(cond):
        @pl.when(cond)
        def _():
            def fore(b, _):
                weighted = scale[pl.ds(b, 1), :] * phi[pl.ds(b, 1), :]
                column = jnp.broadcast_to(weighted, (blk, blk)).T
                for k in range(slots):
                    out = tiles[b, :, k * blk : (k + 1) * blk] * column
                    contrib[b, k : k + 1, :] = jnp.sum(out, axis=0, keepdims=True)
                return 0

            lax.fori_loop(0, own, fore, 0)
            part[...] = lax.dot_general(
                hot[...], contrib[...].reshape(own * slots, blk),
                (((1,), (0,)), ((), ())),
                precision=lax.Precision.HIGHEST, preferred_element_type=jnp.float32,
            )

        each(cond, sum_copy, "start")

    @pl.when(place == 0)
    def _():
        phi[...] = jnp.ones_like(phi)

    @pl.when(place == S - 1)
    def _():
        beta[...] = jnp.ones_like(beta)

    forward(place == 0)
    each(has_next, value_copy, "wait_recv", True)

    @pl.when(has_next)
    def _():
        def back(b, _):
            acc = jnp.zeros((blk, blk), jnp.float32)
            for k in range(slots):
                row = window[pl.ds(ids[k, b], 1), :]
                acc = acc + tiles[b, :, k * blk : (k + 1) * blk] * row
            rows = lax.dot_general(
                jnp.ones((8, blk), jnp.float32), acc, (((1,), (1,)), ((), ())),
                precision=lax.Precision.HIGHEST, preferred_element_type=jnp.float32,
            )
            beta[pl.ds(b, 1), :] = rows[0:1]
            return 0

        lax.fori_loop(0, own, back, 0)
        vals[...] = scale[...] * beta[...]

    each((place >= 1) & has_next, value_copy, "start")
    each(place >= 1, sum_copy, "wait_recv", True)

    @pl.when(place >= 1)
    def _():
        phi[...] = same_in[...]
        phi[pl.ds(own - reach, reach), :] += low_in[...]
        phi[pl.ds(0, reach), :] += high_in[...]

    forward((place >= 1) & has_next)

    @pl.when(place >= 1)
    def _():
        feature_copy(0).wait_send()
        feature_copy(1).wait_send()

    for h in (0, 1):
        @pl.when(has_next & inside[2 * h])
        def _(h=h):
            relay(h).wait_send()

    each(place >= 1, value_copy, "wait_send")
    each(has_next, sum_copy, "wait_send")


def local(features, weights, scales, neighbors):
    dims = features.shape[0]
    slots, own = neighbors.shape
    blk = features.shape[1] // own
    reach = (own + 1) // 2
    wide = own + 2 * reach
    slab = lax.axis_size("cells") // S
    me = lax.axis_index("cells")
    eps = dims * 0.25

    live = (neighbors >= 0).astype(jnp.float32)
    first = (me + slab) * own - reach
    ids = jnp.where(neighbors >= 0, neighbors - first, reach)
    ids = jnp.clip(ids, 0, wide - 1)

    scale = scales.reshape(own, blk)
    smem = pl.BlockSpec(memory_space=pltpu.SMEM)
    vmem = pl.BlockSpec(memory_space=pltpu.VMEM)
    rows = jax.ShapeDtypeStruct((own, blk), jnp.float32)
    at = ids.T.reshape(1, own * slots)
    hot = (at == jnp.arange(wide, dtype=jnp.int32)[:, None]) & (
        live.T.reshape(1, own * slots) > 0
    )
    sem = pltpu.SemaphoreType.DMA((3,))
    beta, phi = pl.pallas_call(
        functools.partial(chain_kernel, slab, eps),
        in_specs=[smem] * 2 + [vmem] * 3,
        out_specs=[vmem, vmem],
        out_shape=[rows, rows],
        scratch_shapes=[
            pltpu.VMEM((own, blk, slots * blk), jnp.float32),
            pltpu.VMEM((dims, wide * blk), jnp.float32),
            pltpu.VMEM((wide, 3 * dims + 16, blk), jnp.bfloat16),
            pltpu.VMEM((wide, blk), jnp.float32),
            pltpu.VMEM((own, blk), jnp.float32),
            pltpu.VMEM((wide, blk), jnp.float32),
            pltpu.VMEM((own, blk), jnp.float32),
            pltpu.VMEM((reach, blk), jnp.float32),
            pltpu.VMEM((reach, blk), jnp.float32),
            pltpu.VMEM((own, slots, blk), jnp.float32),
            sem, sem, sem, sem, sem, sem, sem, sem,
        ],
        compiler_params=pltpu.CompilerParams(
            collective_id=0, has_side_effects=True, vmem_limit_bytes=40 * 1024 * 1024
        ),
    )(ids, live, features, hot.astype(jnp.float32), scale)
    return jnp.log(weights) - jnp.log(phi.reshape(-1)) - jnp.log(beta.reshape(-1))


def solution(mesh):
    placed = (
        P(None, ("groups", "cells")),
        P(("groups", "cells")),
        P(("groups", "cells")),
        P(None, "cells"),
    )
    return jax.shard_map(
        local, mesh=mesh, in_specs=placed, out_specs=P(("groups", "cells")), check_vma=False
    )
```

```python
import functools
import jax
import jax.numpy as jnp
from jax import lax
from jax.experimental import pallas as pl
from jax.experimental.pallas import tpu as pltpu
from jax.sharding import PartitionSpec as P

S = 4
LOG2E = 1.4426950408889634


def split(x):
    hi = x.astype(jnp.bfloat16)
    lo = (x - hi.astype(jnp.float32)).astype(jnp.bfloat16)
    return hi, lo


def stacked(x, eps, own):
    norm = jnp.sum(x * x, axis=0, keepdims=True) * (-LOG2E / eps)
    a = norm.astype(jnp.bfloat16).astype(jnp.float32)
    b = (norm - a).astype(jnp.bfloat16).astype(jnp.float32)
    c = norm - a - b
    row = lax.broadcasted_iota(jnp.int32, (16, x.shape[1]), 0)
    if not own:
        row = row - 3
    tail = jnp.where(row == 0, a, jnp.where(row == 1, b, jnp.where(row == 2, c, 0.0)))
    ones = (row >= 3) & (row < 6) if own else (row < 0)
    tail = jnp.where(ones, 1.0, tail).astype(jnp.bfloat16)
    hi, lo = split(x * (2.0 * LOG2E / eps) if own else x)
    parts = [hi, lo, hi, tail] if own else [hi, hi, lo, tail]
    return jnp.concatenate(parts, axis=0)


def blocks(low, high, body, at_once):
    if (high - low) % at_once:
        at_once = 1

    def step(i, _):
        for j in range(at_once):
            body(low + i * at_once + j, 0)
        return 0

    lax.fori_loop(0, (high - low) // at_once, step, 0)


def chain_kernel(slab, eps, ids, live, feats, hot, scale, beta, phi,
                 tiles, fwin, stack,
                 window, vals, part, same_in, low_in, high_in, contrib,
                 fsend, frecv, rsend, rrecv, vsend, vrecv, psend, precv):
    me = lax.axis_index("cells")
    place, spot = me // slab, me % slab
    slots = ids.shape[0]
    own, blk = scale.shape
    wide = window.shape[0]
    reach = (wide - own) // 2
    inside = (spot > 0, spot >= 0, spot < slab - 1)

    window[...] = jnp.zeros_like(window)
    low_in[...] = jnp.zeros_like(low_in)
    high_in[...] = jnp.zeros_like(high_in)
    vals[...] = scale[...]
    edge, middle = reach * blk, own * blk
    fwin[:, :edge] = jnp.zeros((fwin.shape[0], edge), jnp.float32)
    fwin[:, edge + middle :] = jnp.zeros((fwin.shape[0], edge), jnp.float32)

    barrier = pltpu.get_barrier_semaphore()
    for near, step in ((place > 0, -slab), (place < S - 1, slab)):
        for o in (-1, 0, 1):
            @pl.when(near & inside[o + 1])
            def _(step=step, o=o):
                pl.semaphore_signal(
                    barrier, inc=1, device_id={"cells": me + step + o},
                    device_id_type=pl.DeviceIdType.MESH,
                )
    for o in (-1, 1):
        @pl.when(inside[o + 1])
        def _(o=o):
            pl.semaphore_signal(
                barrier, inc=1, device_id={"cells": me + o},
                device_id_type=pl.DeviceIdType.MESH,
            )
    sides = jnp.where(place > 0, 1, 0) + jnp.where(place < S - 1, 1, 0)
    near = 1 + jnp.where(inside[0], 1, 0) + jnp.where(inside[2], 1, 0)
    pl.semaphore_wait(barrier, sides * near + near - 1)

    def copy(src, dst, send, recv, target):
        return pltpu.make_async_remote_copy(
            src_ref=src, dst_ref=dst, send_sem=send, recv_sem=recv,
            device_id={"cells": target}, device_id_type=pl.DeviceIdType.MESH,
        )

    value_parts = {
        -1: (vals.at[pl.ds(0, reach)], window.at[pl.ds(reach + own, reach)]),
        0: (vals, window.at[pl.ds(reach, own)]),
        1: (vals.at[pl.ds(own - reach, reach)], window.at[pl.ds(0, reach)]),
    }
    sum_parts = {
        -1: (part.at[pl.ds(0, reach)], low_in),
        0: (part.at[pl.ds(reach, own)], same_in),
        1: (part.at[pl.ds(reach + own, reach)], high_in),
    }

    def feature_copy(h):
        return copy(
            feats.at[:, pl.ds(h * edge, edge)], fwin.at[:, pl.ds((h + 1) * edge, edge)],
            fsend.at[h], frecv.at[h], me - slab,
        )

    def relay(h):
        return copy(
            fwin.at[:, pl.ds((h + 1) * edge, edge)],
            fwin.at[:, pl.ds((1 - h) * (edge + middle), edge)],
            rsend.at[h], rrecv.at[h], me + 2 * h - 1,
        )

    def value_copy(o):
        src, dst = value_parts[o]
        return copy(src, dst, vsend.at[o + 1], vrecv.at[o + 1], me - slab + o)

    def sum_copy(o):
        src, dst = sum_parts[o]
        return copy(src, dst, psend.at[o + 1], precv.at[o + 1], me + slab + o)

    def each(cond, make, act, flip=False):
        for o in (-1, 0, 1):
            @pl.when(cond & inside[(-o if flip else o) + 1])
            def _(o=o):
                getattr(make(o), act)()

    @pl.when(place >= 1)
    def _():
        feature_copy(0).start()
        feature_copy(1).start()

    each(place == S - 1, value_copy, "start")
    has_next = place < S - 1

    def lanes(b):
        return pl.ds(pl.multiple_of(b * blk, blk), blk)

    def prepare(w, _):
        stack[w] = stacked(fwin[:, lanes(w)], eps, False)
        return 0

    for h in (0, 1):
        @pl.when(has_next)
        def _(h=h):
            feature_copy(h).wait_recv()

        @pl.when(has_next & inside[2 * h])
        def _(h=h):
            relay(h).start()

        @pl.when(has_next)
        def _(h=h):
            blocks((h + 1) * reach, (h + 2) * reach, prepare, 2)

    for h in (0, 1):
        @pl.when(has_next & inside[2 - 2 * h])
        def _(h=h):
            relay(h).wait_recv()

    @pl.when(has_next)
    def _():
        blocks(0, reach, prepare, 2)
        blocks(reach + own, wide, prepare, 2)

        def build(b, _):
            mine = stacked(feats[:, lanes(b)], eps, True).T
            for k in range(0, slots, 2):
                theirs = jnp.concatenate(
                    [stack[ids[k, b]], stack[ids[k + 1, b]]], axis=1
                )
                expo = lax.dot_general(
                    mine, theirs, (((1,), (0,)), ((), ())),
                    preferred_element_type=jnp.float32,
                )
                tile = jnp.exp2(expo)
                for i in (0, 1):
                    tiles[b, :, (k + i) * blk : (k + i + 1) * blk] = (
                        tile[:, i * blk : (i + 1) * blk] * live[k + i, b]
                    )
            return 0

        blocks(0, own, build, 2)

    def forward(cond):
        @pl.when(cond)
        def _():
            def fore(b, _):
                weighted = scale[pl.ds(b, 1), :] * phi[pl.ds(b, 1), :]
                column = jnp.broadcast_to(weighted, (blk, blk)).T
                for k in range(slots):
                    out = tiles[b, :, k * blk : (k + 1) * blk] * column
                    contrib[b, k : k + 1, :] = jnp.sum(out, axis=0, keepdims=True)
                return 0

            blocks(0, own, fore, 2)
            part[...] = lax.dot_general(
                hot[...], contrib[...].reshape(own * slots, blk),
                (((1,), (0,)), ((), ())),
                precision=lax.Precision.HIGHEST, preferred_element_type=jnp.float32,
            )

        each(cond, sum_copy, "start")

    @pl.when(place == 0)
    def _():
        phi[...] = jnp.ones_like(phi)

    @pl.when(place == S - 1)
    def _():
        beta[...] = jnp.ones_like(beta)

    forward(place == 0)
    each(has_next, value_copy, "wait_recv", True)

    @pl.when(has_next)
    def _():
        def back(b, _):
            acc = jnp.zeros((blk, blk), jnp.float32)
            for k in range(slots):
                row = window[pl.ds(ids[k, b], 1), :]
                acc = acc + tiles[b, :, k * blk : (k + 1) * blk] * row
            rows = lax.dot_general(
                jnp.ones((8, blk), jnp.float32), acc, (((1,), (1,)), ((), ())),
                precision=lax.Precision.HIGHEST, preferred_element_type=jnp.float32,
            )
            beta[pl.ds(b, 1), :] = rows[0:1]
            return 0

        blocks(0, own, back, 4)
        vals[...] = scale[...] * beta[...]

    each((place >= 1) & has_next, value_copy, "start")
    each(place >= 1, sum_copy, "wait_recv", True)

    @pl.when(place >= 1)
    def _():
        phi[...] = same_in[...]
        phi[pl.ds(own - reach, reach), :] += low_in[...]
        phi[pl.ds(0, reach), :] += high_in[...]

    forward((place >= 1) & has_next)

    @pl.when(place >= 1)
    def _():
        feature_copy(0).wait_send()
        feature_copy(1).wait_send()

    for h in (0, 1):
        @pl.when(has_next & inside[2 * h])
        def _(h=h):
            relay(h).wait_send()

    each(place >= 1, value_copy, "wait_send")
    each(has_next, sum_copy, "wait_send")


def local(features, weights, scales, neighbors):
    dims = features.shape[0]
    slots, own = neighbors.shape
    blk = features.shape[1] // own
    reach = (own + 1) // 2
    wide = own + 2 * reach
    slab = lax.axis_size("cells") // S
    me = lax.axis_index("cells")
    eps = dims * 0.25

    live = (neighbors >= 0).astype(jnp.float32)
    first = (me + slab) * own - reach
    ids = jnp.where(neighbors >= 0, neighbors - first, reach)
    ids = jnp.clip(ids, 0, wide - 1)

    scale = scales.reshape(own, blk)
    smem = pl.BlockSpec(memory_space=pltpu.SMEM)
    vmem = pl.BlockSpec(memory_space=pltpu.VMEM)
    rows = jax.ShapeDtypeStruct((own, blk), jnp.float32)
    at = ids.T.reshape(1, own * slots)
    hot = (at == jnp.arange(wide, dtype=jnp.int32)[:, None]) & (
        live.T.reshape(1, own * slots) > 0
    )
    sem = pltpu.SemaphoreType.DMA((3,))
    beta, phi = pl.pallas_call(
        functools.partial(chain_kernel, slab, eps),
        in_specs=[smem] * 2 + [vmem] * 3,
        out_specs=[vmem, vmem],
        out_shape=[rows, rows],
        scratch_shapes=[
            pltpu.VMEM((own, blk, slots * blk), jnp.float32),
            pltpu.VMEM((dims, wide * blk), jnp.float32),
            pltpu.VMEM((wide, 3 * dims + 16, blk), jnp.bfloat16),
            pltpu.VMEM((wide, blk), jnp.float32),
            pltpu.VMEM((own, blk), jnp.float32),
            pltpu.VMEM((wide, blk), jnp.float32),
            pltpu.VMEM((own, blk), jnp.float32),
            pltpu.VMEM((reach, blk), jnp.float32),
            pltpu.VMEM((reach, blk), jnp.float32),
            pltpu.VMEM((own, slots, blk), jnp.float32),
            sem, sem, sem, sem, sem, sem, sem, sem,
        ],
        compiler_params=pltpu.CompilerParams(
            collective_id=0, has_side_effects=True, vmem_limit_bytes=40 * 1024 * 1024
        ),
    )(ids, live, features, hot.astype(jnp.float32), scale)
    return jnp.log(weights) - jnp.log(phi.reshape(-1)) - jnp.log(beta.reshape(-1))


def solution(mesh):
    placed = (
        P(None, ("groups", "cells")),
        P(("groups", "cells")),
        P(("groups", "cells")),
        P(None, "cells"),
    )
    return jax.shard_map(
        local, mesh=mesh, in_specs=placed, out_specs=P(("groups", "cells")), check_vma=False
    )
```

```python
import functools
import jax
import jax.numpy as jnp
from jax import lax
from jax.experimental import pallas as pl
from jax.experimental.pallas import tpu as pltpu
from jax.sharding import PartitionSpec as P

S = 4
LOG2E = 1.4426950408889634


def split(x):
    hi = x.astype(jnp.bfloat16)
    lo = (x - hi.astype(jnp.float32)).astype(jnp.bfloat16)
    return hi, lo


def stacked(x, eps, own):
    norm = jnp.sum(x * x, axis=0, keepdims=True) * (-LOG2E / eps)
    a = norm.astype(jnp.bfloat16).astype(jnp.float32)
    b = (norm - a).astype(jnp.bfloat16).astype(jnp.float32)
    c = norm - a - b
    row = lax.broadcasted_iota(jnp.int32, (16, x.shape[1]), 0)
    if not own:
        row = row - 3
    tail = jnp.where(row == 0, a, jnp.where(row == 1, b, jnp.where(row == 2, c, 0.0)))
    ones = (row >= 3) & (row < 6) if own else (row < 0)
    tail = jnp.where(ones, 1.0, tail).astype(jnp.bfloat16)
    hi, lo = split(x * (2.0 * LOG2E / eps) if own else x)
    parts = [hi, lo, hi, tail] if own else [hi, hi, lo, tail]
    return jnp.concatenate(parts, axis=0)


def blocks(low, high, body, at_once):
    if (high - low) % at_once:
        at_once = 1

    def step(i, _):
        for j in range(at_once):
            body(low + i * at_once + j, 0)
        return 0

    lax.fori_loop(0, (high - low) // at_once, step, 0)


def chain_kernel(slab, eps, ids, live, feats, hot, scale, beta, phi,
                 tiles, fwin, stack,
                 window, vals, part, same_in, low_in, high_in, contrib,
                 fsend, frecv, rsend, rrecv, vsend, vrecv, psend, precv):
    me = lax.axis_index("cells")
    place, spot = me // slab, me % slab
    slots = ids.shape[0]
    own, blk = scale.shape
    wide = window.shape[0]
    reach = (wide - own) // 2
    inside = (spot > 0, spot >= 0, spot < slab - 1)

    window[...] = jnp.zeros_like(window)
    low_in[...] = jnp.zeros_like(low_in)
    high_in[...] = jnp.zeros_like(high_in)
    vals[...] = scale[...]
    edge, middle = reach * blk, own * blk
    fwin[:, :edge] = jnp.zeros((fwin.shape[0], edge), jnp.float32)
    fwin[:, edge + middle :] = jnp.zeros((fwin.shape[0], edge), jnp.float32)

    barrier = pltpu.get_barrier_semaphore()
    for near, step in ((place > 0, -slab), (place < S - 1, slab)):
        for o in (-1, 0, 1):
            @pl.when(near & inside[o + 1])
            def _(step=step, o=o):
                pl.semaphore_signal(
                    barrier, inc=1, device_id={"cells": me + step + o},
                    device_id_type=pl.DeviceIdType.MESH,
                )
    for o in (-1, 1):
        @pl.when(inside[o + 1])
        def _(o=o):
            pl.semaphore_signal(
                barrier, inc=1, device_id={"cells": me + o},
                device_id_type=pl.DeviceIdType.MESH,
            )
    sides = jnp.where(place > 0, 1, 0) + jnp.where(place < S - 1, 1, 0)
    near = 1 + jnp.where(inside[0], 1, 0) + jnp.where(inside[2], 1, 0)
    pl.semaphore_wait(barrier, sides * near + near - 1)

    def copy(src, dst, send, recv, target):
        return pltpu.make_async_remote_copy(
            src_ref=src, dst_ref=dst, send_sem=send, recv_sem=recv,
            device_id={"cells": target}, device_id_type=pl.DeviceIdType.MESH,
        )

    value_parts = {
        -1: (vals.at[pl.ds(0, reach)], window.at[pl.ds(reach + own, reach)]),
        0: (vals, window.at[pl.ds(reach, own)]),
        1: (vals.at[pl.ds(own - reach, reach)], window.at[pl.ds(0, reach)]),
    }
    sum_parts = {
        -1: (part.at[pl.ds(0, reach)], low_in),
        0: (part.at[pl.ds(reach, own)], same_in),
        1: (part.at[pl.ds(reach + own, reach)], high_in),
    }

    halves = 2 if reach % 2 == 0 else 1
    pieces = 2 * halves
    count = reach // halves
    size = count * blk

    def feature_copy(p):
        return copy(
            feats.at[:, pl.ds(p * size, size)],
            fwin.at[:, pl.ds(edge + p * size, size)],
            fsend.at[p], frecv.at[p], me - slab,
        )

    def landing(p):
        return p * size + edge + middle if p < halves else p * size - edge

    def relay(p):
        return copy(
            fwin.at[:, pl.ds(edge + p * size, size)],
            fwin.at[:, pl.ds(landing(p), size)],
            rsend.at[p], rrecv.at[p], me - 1 if p < halves else me + 1,
        )

    def value_copy(o):
        src, dst = value_parts[o]
        return copy(src, dst, vsend.at[o + 1], vrecv.at[o + 1], me - slab + o)

    def sum_copy(o):
        src, dst = sum_parts[o]
        return copy(src, dst, psend.at[o + 1], precv.at[o + 1], me + slab + o)

    def each(cond, make, act, flip=False):
        for o in (-1, 0, 1):
            @pl.when(cond & inside[(-o if flip else o) + 1])
            def _(o=o):
                getattr(make(o), act)()

    @pl.when(place >= 1)
    def _():
        for p in range(pieces):
            feature_copy(p).start()

    each(place == S - 1, value_copy, "start")
    has_next = place < S - 1

    def lanes(b):
        return pl.ds(pl.multiple_of(b * blk, blk), blk)

    def prepare(w, _):
        stack[w] = stacked(fwin[:, lanes(w)], eps, False)
        return 0

    for p in range(pieces):
        @pl.when(has_next)
        def _(p=p):
            feature_copy(p).wait_recv()

        @pl.when(has_next & inside[0 if p < halves else 2])
        def _(p=p):
            relay(p).start()

        @pl.when(has_next)
        def _(p=p):
            blocks(reach + p * count, reach + (p + 1) * count, prepare, 4)

    for p in range(pieces):
        @pl.when(has_next & inside[2 if p < halves else 0])
        def _(p=p):
            relay(p).wait_recv()

        @pl.when(has_next)
        def _(p=p):
            blocks(landing(p) // blk, landing(p) // blk + count, prepare, 4)

    @pl.when(has_next)
    def _():
        def build(b, _):
            mine = stacked(feats[:, lanes(b)], eps, True).T
            for k in range(0, slots, 2):
                theirs = jnp.concatenate(
                    [stack[ids[k, b]], stack[ids[k + 1, b]]], axis=1
                )
                expo = lax.dot_general(
                    mine, theirs, (((1,), (0,)), ((), ())),
                    preferred_element_type=jnp.float32,
                )
                tile = jnp.exp2(expo)
                for i in (0, 1):
                    tiles[b, :, (k + i) * blk : (k + i + 1) * blk] = (
                        tile[:, i * blk : (i + 1) * blk] * live[k + i, b]
                    )
            return 0

        blocks(0, own, build, 4)

    def forward(cond):
        @pl.when(cond)
        def _():
            def fore(b, _):
                weighted = scale[pl.ds(b, 1), :] * phi[pl.ds(b, 1), :]
                column = jnp.broadcast_to(weighted, (blk, blk)).T
                for k in range(slots):
                    out = tiles[b, :, k * blk : (k + 1) * blk] * column
                    contrib[b, k : k + 1, :] = jnp.sum(out, axis=0, keepdims=True)
                return 0

            blocks(0, own, fore, 4)
            part[...] = lax.dot_general(
                hot[...], contrib[...].reshape(own * slots, blk),
                (((1,), (0,)), ((), ())),
                precision=lax.Precision.HIGHEST, preferred_element_type=jnp.float32,
            )

        each(cond, sum_copy, "start")

    @pl.when(place == 0)
    def _():
        phi[...] = jnp.ones_like(phi)

    @pl.when(place == S - 1)
    def _():
        beta[...] = jnp.ones_like(beta)

    forward(place == 0)
    each(has_next, value_copy, "wait_recv", True)

    @pl.when(has_next)
    def _():
        def back(b, _):
            acc = jnp.zeros((blk, blk), jnp.float32)
            for k in range(slots):
                row = window[pl.ds(ids[k, b], 1), :]
                acc = acc + tiles[b, :, k * blk : (k + 1) * blk] * row
            rows = lax.dot_general(
                jnp.ones((8, blk), jnp.float32), acc, (((1,), (1,)), ((), ())),
                precision=lax.Precision.HIGHEST, preferred_element_type=jnp.float32,
            )
            beta[pl.ds(b, 1), :] = rows[0:1]
            return 0

        blocks(0, own, back, 4)
        vals[...] = scale[...] * beta[...]

    each((place >= 1) & has_next, value_copy, "start")
    each(place >= 1, sum_copy, "wait_recv", True)

    @pl.when(place >= 1)
    def _():
        phi[...] = same_in[...]
        phi[pl.ds(own - reach, reach), :] += low_in[...]
        phi[pl.ds(0, reach), :] += high_in[...]

    forward((place >= 1) & has_next)

    @pl.when(place >= 1)
    def _():
        for p in range(pieces):
            feature_copy(p).wait_send()

    for p in range(pieces):
        @pl.when(has_next & inside[0 if p < halves else 2])
        def _(p=p):
            relay(p).wait_send()

    each(place >= 1, value_copy, "wait_send")
    each(has_next, sum_copy, "wait_send")


def local(features, weights, scales, neighbors):
    dims = features.shape[0]
    slots, own = neighbors.shape
    blk = features.shape[1] // own
    reach = (own + 1) // 2
    wide = own + 2 * reach
    slab = lax.axis_size("cells") // S
    me = lax.axis_index("cells")
    eps = dims * 0.25

    live = (neighbors >= 0).astype(jnp.float32)
    first = (me + slab) * own - reach
    ids = jnp.where(neighbors >= 0, neighbors - first, reach)
    ids = jnp.clip(ids, 0, wide - 1)

    scale = scales.reshape(own, blk)
    smem = pl.BlockSpec(memory_space=pltpu.SMEM)
    vmem = pl.BlockSpec(memory_space=pltpu.VMEM)
    rows = jax.ShapeDtypeStruct((own, blk), jnp.float32)
    at = ids.T.reshape(1, own * slots)
    hot = (at == jnp.arange(wide, dtype=jnp.int32)[:, None]) & (
        live.T.reshape(1, own * slots) > 0
    )
    sem = pltpu.SemaphoreType.DMA((4,))
    beta, phi = pl.pallas_call(
        functools.partial(chain_kernel, slab, eps),
        in_specs=[smem] * 2 + [vmem] * 3,
        out_specs=[vmem, vmem],
        out_shape=[rows, rows],
        scratch_shapes=[
            pltpu.VMEM((own, blk, slots * blk), jnp.float32),
            pltpu.VMEM((dims, wide * blk), jnp.float32),
            pltpu.VMEM((wide, 3 * dims + 16, blk), jnp.bfloat16),
            pltpu.VMEM((wide, blk), jnp.float32),
            pltpu.VMEM((own, blk), jnp.float32),
            pltpu.VMEM((wide, blk), jnp.float32),
            pltpu.VMEM((own, blk), jnp.float32),
            pltpu.VMEM((reach, blk), jnp.float32),
            pltpu.VMEM((reach, blk), jnp.float32),
            pltpu.VMEM((own, slots, blk), jnp.float32),
            sem, sem, sem, sem, sem, sem, sem, sem,
        ],
        compiler_params=pltpu.CompilerParams(
            collective_id=0, has_side_effects=True, vmem_limit_bytes=40 * 1024 * 1024
        ),
    )(ids, live, features, hot.astype(jnp.float32), scale)
    return jnp.log(weights) - jnp.log(phi.reshape(-1)) - jnp.log(beta.reshape(-1))


def solution(mesh):
    placed = (
        P(None, ("groups", "cells")),
        P(("groups", "cells")),
        P(("groups", "cells")),
        P(None, "cells"),
    )
    return jax.shard_map(
        local, mesh=mesh, in_specs=placed, out_specs=P(("groups", "cells")), check_vma=False
    )
```

```python
import functools
import jax
import jax.numpy as jnp
from jax import lax
from jax.experimental import pallas as pl
from jax.experimental.pallas import tpu as pltpu
from jax.sharding import PartitionSpec as P

S = 4
LOG2E = 1.4426950408889634


def split(x):
    hi = x.astype(jnp.bfloat16)
    lo = (x - hi.astype(jnp.float32)).astype(jnp.bfloat16)
    return hi, lo


def stacked(x, eps, own):
    norm = jnp.sum(x * x, axis=0, keepdims=True) * (-LOG2E / eps)
    a = norm.astype(jnp.bfloat16).astype(jnp.float32)
    b = (norm - a).astype(jnp.bfloat16).astype(jnp.float32)
    c = norm - a - b
    row = lax.broadcasted_iota(jnp.int32, (16, x.shape[1]), 0)
    if not own:
        row = row - 3
    tail = jnp.where(row == 0, a, jnp.where(row == 1, b, jnp.where(row == 2, c, 0.0)))
    ones = (row >= 3) & (row < 6) if own else (row < 0)
    tail = jnp.where(ones, 1.0, tail).astype(jnp.bfloat16)
    hi, lo = split(x * (2.0 * LOG2E / eps) if own else x)
    parts = [hi, lo, hi, tail] if own else [hi, hi, lo, tail]
    return jnp.concatenate(parts, axis=0)


def blocks(low, high, body, at_once):
    if (high - low) % at_once:
        at_once = 1

    def step(i, _):
        for j in range(at_once):
            body(low + i * at_once + j, 0)
        return 0

    lax.fori_loop(0, (high - low) // at_once, step, 0)


def chain_kernel(slab, eps, ids, live, feats, hot, scale, beta, phi,
                 tiles, fwin, stack,
                 window, vals, part, same_in, low_in, high_in, contrib,
                 fsend, frecv, rsend, rrecv, vsend, vrecv, psend, precv):
    me = lax.axis_index("cells")
    place, spot = me // slab, me % slab
    slots = ids.shape[0]
    own, blk = scale.shape
    wide = window.shape[0]
    reach = (wide - own) // 2
    inside = (spot > 0, spot >= 0, spot < slab - 1)

    window[...] = jnp.zeros_like(window)
    low_in[...] = jnp.zeros_like(low_in)
    high_in[...] = jnp.zeros_like(high_in)
    vals[...] = scale[...]
    edge, middle = reach * blk, own * blk
    fwin[:, :edge] = jnp.zeros((fwin.shape[0], edge), jnp.float32)
    fwin[:, edge + middle :] = jnp.zeros((fwin.shape[0], edge), jnp.float32)

    barrier = pltpu.get_barrier_semaphore()
    for near, step in ((place > 0, -slab), (place < S - 1, slab)):
        for o in (-1, 0, 1):
            @pl.when(near & inside[o + 1])
            def _(step=step, o=o):
                pl.semaphore_signal(
                    barrier, inc=1, device_id={"cells": me + step + o},
                    device_id_type=pl.DeviceIdType.MESH,
                )
    for o in (-1, 1):
        @pl.when(inside[o + 1])
        def _(o=o):
            pl.semaphore_signal(
                barrier, inc=1, device_id={"cells": me + o},
                device_id_type=pl.DeviceIdType.MESH,
            )
    sides = jnp.where(place > 0, 1, 0) + jnp.where(place < S - 1, 1, 0)
    near = 1 + jnp.where(inside[0], 1, 0) + jnp.where(inside[2], 1, 0)
    pl.semaphore_wait(barrier, sides * near + near - 1)

    def copy(src, dst, send, recv, target):
        return pltpu.make_async_remote_copy(
            src_ref=src, dst_ref=dst, send_sem=send, recv_sem=recv,
            device_id={"cells": target}, device_id_type=pl.DeviceIdType.MESH,
        )

    value_parts = {
        -1: (vals.at[pl.ds(0, reach)], window.at[pl.ds(reach + own, reach)]),
        0: (vals, window.at[pl.ds(reach, own)]),
        1: (vals.at[pl.ds(own - reach, reach)], window.at[pl.ds(0, reach)]),
    }
    sum_parts = {
        -1: (part.at[pl.ds(0, reach)], low_in),
        0: (part.at[pl.ds(reach, own)], same_in),
        1: (part.at[pl.ds(reach + own, reach)], high_in),
    }

    halves = 4 if reach % 4 == 0 else 1
    pieces = 2 * halves
    count = reach // halves
    size = count * blk

    def feature_copy(p):
        return copy(
            feats.at[:, pl.ds(p * size, size)],
            fwin.at[:, pl.ds(edge + p * size, size)],
            fsend.at[p], frecv.at[p], me - slab,
        )

    def landing(p):
        return p * size + edge + middle if p < halves else p * size - edge

    def relay(p):
        return copy(
            fwin.at[:, pl.ds(edge + p * size, size)],
            fwin.at[:, pl.ds(landing(p), size)],
            rsend.at[p], rrecv.at[p], me - 1 if p < halves else me + 1,
        )

    def value_copy(o):
        src, dst = value_parts[o]
        return copy(src, dst, vsend.at[o + 1], vrecv.at[o + 1], me - slab + o)

    def sum_copy(o):
        src, dst = sum_parts[o]
        return copy(src, dst, psend.at[o + 1], precv.at[o + 1], me + slab + o)

    def each(cond, make, act, flip=False):
        for o in (-1, 0, 1):
            @pl.when(cond & inside[(-o if flip else o) + 1])
            def _(o=o):
                getattr(make(o), act)()

    @pl.when(place >= 1)
    def _():
        for p in range(pieces):
            feature_copy(p).start()

    each(place == S - 1, value_copy, "start")
    has_next = place < S - 1

    def lanes(b):
        return pl.ds(pl.multiple_of(b * blk, blk), blk)

    def prepare(w, _):
        stack[w] = stacked(fwin[:, lanes(w)], eps, False)
        return 0

    for p in range(pieces):
        @pl.when(has_next)
        def _(p=p):
            feature_copy(p).wait_recv()

        @pl.when(has_next & inside[0 if p < halves else 2])
        def _(p=p):
            relay(p).start()

        @pl.when(has_next)
        def _(p=p):
            blocks(reach + p * count, reach + (p + 1) * count, prepare, 4)

    for p in range(pieces):
        @pl.when(has_next & inside[2 if p < halves else 0])
        def _(p=p):
            relay(p).wait_recv()

        @pl.when(has_next)
        def _(p=p):
            blocks(landing(p) // blk, landing(p) // blk + count, prepare, 4)

    @pl.when(has_next)
    def _():
        def build(b, _):
            mine = stacked(feats[:, lanes(b)], eps, True).T
            for k in range(0, slots, 2):
                theirs = jnp.concatenate(
                    [stack[ids[k, b]], stack[ids[k + 1, b]]], axis=1
                )
                expo = lax.dot_general(
                    mine, theirs, (((1,), (0,)), ((), ())),
                    preferred_element_type=jnp.float32,
                )
                tile = jnp.exp2(expo)
                for i in (0, 1):
                    tiles[b, :, (k + i) * blk : (k + i + 1) * blk] = (
                        tile[:, i * blk : (i + 1) * blk] * live[k + i, b]
                    )
            return 0

        blocks(0, own, build, 8)

    def forward(cond):
        @pl.when(cond)
        def _():
            def fore(b, _):
                weighted = scale[pl.ds(b, 1), :] * phi[pl.ds(b, 1), :]
                column = jnp.broadcast_to(weighted, (blk, blk)).T
                for k in range(slots):
                    out = tiles[b, :, k * blk : (k + 1) * blk] * column
                    contrib[b, k : k + 1, :] = jnp.sum(out, axis=0, keepdims=True)
                return 0

            blocks(0, own, fore, 8)
            part[...] = lax.dot_general(
                hot[...], contrib[...].reshape(own * slots, blk),
                (((1,), (0,)), ((), ())),
                precision=lax.Precision.HIGHEST, preferred_element_type=jnp.float32,
            )

        each(cond, sum_copy, "start")

    @pl.when(place == 0)
    def _():
        phi[...] = jnp.ones_like(phi)

    @pl.when(place == S - 1)
    def _():
        beta[...] = jnp.ones_like(beta)

    forward(place == 0)
    each(has_next, value_copy, "wait_recv", True)

    @pl.when(has_next)
    def _():
        def back(b, _):
            acc = jnp.zeros((blk, blk), jnp.float32)
            for k in range(slots):
                row = window[pl.ds(ids[k, b], 1), :]
                acc = acc + tiles[b, :, k * blk : (k + 1) * blk] * row
            rows = lax.dot_general(
                jnp.ones((8, blk), jnp.float32), acc, (((1,), (1,)), ((), ())),
                precision=lax.Precision.HIGHEST, preferred_element_type=jnp.float32,
            )
            beta[pl.ds(b, 1), :] = rows[0:1]
            return 0

        blocks(0, own, back, 8)
        vals[...] = scale[...] * beta[...]

    each((place >= 1) & has_next, value_copy, "start")
    each(place >= 1, sum_copy, "wait_recv", True)

    @pl.when(place >= 1)
    def _():
        phi[...] = same_in[...]
        phi[pl.ds(own - reach, reach), :] += low_in[...]
        phi[pl.ds(0, reach), :] += high_in[...]

    forward((place >= 1) & has_next)

    @pl.when(place >= 1)
    def _():
        for p in range(pieces):
            feature_copy(p).wait_send()

    for p in range(pieces):
        @pl.when(has_next & inside[0 if p < halves else 2])
        def _(p=p):
            relay(p).wait_send()

    each(place >= 1, value_copy, "wait_send")
    each(has_next, sum_copy, "wait_send")


def local(features, weights, scales, neighbors):
    dims = features.shape[0]
    slots, own = neighbors.shape
    blk = features.shape[1] // own
    reach = (own + 1) // 2
    wide = own + 2 * reach
    slab = lax.axis_size("cells") // S
    me = lax.axis_index("cells")
    eps = dims * 0.25

    live = (neighbors >= 0).astype(jnp.float32)
    first = (me + slab) * own - reach
    ids = jnp.where(neighbors >= 0, neighbors - first, reach)
    ids = jnp.clip(ids, 0, wide - 1)

    scale = scales.reshape(own, blk)
    smem = pl.BlockSpec(memory_space=pltpu.SMEM)
    vmem = pl.BlockSpec(memory_space=pltpu.VMEM)
    rows = jax.ShapeDtypeStruct((own, blk), jnp.float32)
    at = ids.T.reshape(1, own * slots)
    hot = (at == jnp.arange(wide, dtype=jnp.int32)[:, None]) & (
        live.T.reshape(1, own * slots) > 0
    )
    sem = pltpu.SemaphoreType.DMA((8,))
    beta, phi = pl.pallas_call(
        functools.partial(chain_kernel, slab, eps),
        in_specs=[smem] * 2 + [vmem] * 3,
        out_specs=[vmem, vmem],
        out_shape=[rows, rows],
        scratch_shapes=[
            pltpu.VMEM((own, blk, slots * blk), jnp.float32),
            pltpu.VMEM((dims, wide * blk), jnp.float32),
            pltpu.VMEM((wide, 3 * dims + 16, blk), jnp.bfloat16),
            pltpu.VMEM((wide, blk), jnp.float32),
            pltpu.VMEM((own, blk), jnp.float32),
            pltpu.VMEM((wide, blk), jnp.float32),
            pltpu.VMEM((own, blk), jnp.float32),
            pltpu.VMEM((reach, blk), jnp.float32),
            pltpu.VMEM((reach, blk), jnp.float32),
            pltpu.VMEM((own, slots, blk), jnp.float32),
            sem, sem, sem, sem, sem, sem, sem, sem,
        ],
        compiler_params=pltpu.CompilerParams(
            collective_id=0, has_side_effects=True, vmem_limit_bytes=40 * 1024 * 1024
        ),
    )(ids, live, features, hot.astype(jnp.float32), scale)
    return jnp.log(weights) - jnp.log(phi.reshape(-1)) - jnp.log(beta.reshape(-1))


def solution(mesh):
    placed = (
        P(None, ("groups", "cells")),
        P(("groups", "cells")),
        P(("groups", "cells")),
        P(None, "cells"),
    )
    return jax.shard_map(
        local, mesh=mesh, in_specs=placed, out_specs=P(("groups", "cells")), check_vma=False
    )
```
